128 devices in a mesh: gx: 4 (over z), gy: 4 (over x), gz: 8 (over y, core).
Axes of the slice: x: 4, y: 4, z: 4, core: 2. Of those that a mesh axis runs over, the one named last changes fastest.
Arguments:
- field: float32 [4, 256, 512, 1024], P(None, 'gx', 'gz', 'gy'), may hold values from -6 to 6
- basis_two: float32 [1024, 64], P('gy'), may hold values from -0.1875 to 0.1875
- basis_three: float32 [512, 64], P('gz'), may hold values from -0.25 to 0.25
Outputs:
- projected: float32 [256, 16384], P('gx', ('gy', 'gz'))
- gram: float32 [256, 256], P('gx')
The draws below stay inside these ranges and needn't reach their ends.
All inputs are finite; a program needn't handle non-finite values.
Results may differ from the reference program's by a relative error of at most 0.000071.
Values sent between devices are 32-bit elements; how exact they have to be, the bound alone decides.
No kernel may reach another device: no remote copies, remote signals or barrier semaphores. Data moves between devices by JAX's collectives and lax.ppermute only.
A program may use at most 128 MiB of HBM per device.

```python
import jax
import jax.numpy as jnp
from jax import lax

V = 4
R = 64
N1 = 256
N2 = 1024
N3 = 512
K = 16384


def block_levels(stream_key, dims, split, smallest, top_value):
    level, own = 1.0, jax.random.fold_in(stream_key, 6)
    for axis_at, shards_of in split:
        heights = jnp.exp(jax.random.uniform(jax.random.fold_in(own, axis_at), (shards_of,), jnp.float32, smallest / len(split), top_value / len(split)))
        level = level * jnp.repeat(heights, dims[axis_at] // shards_of).reshape([-1 if axis == axis_at else 1 for axis in range(len(dims))])
    return level


def scatter_about(stream_key, shape, width, limit, cuts=(), held_as=jnp.bfloat16):
    values = jax.random.normal(stream_key, shape, jnp.float32) * width
    if len(cuts) > 0:
        values = block_levels(stream_key, shape, cuts, -0.22, 0.18) * values
    return jnp.clip(values, min=-limit, max=limit).astype(held_as)


def setup_inputs(seed: int = 0) -> dict:
    splits = jax.random.split(jax.random.key(seed), 4)
    field = scatter_about(splits[0], (V, N1, N3, N2), 1.0, 6.0, ((1, 4), (2, 8), (3, 4)), jnp.float32)
    basis_two = scatter_about(splits[1], (N2, R), N2 ** -0.5, 0.1875, ((0, 4),), jnp.float32)
    basis_three = scatter_about(splits[2], (N3, R), N3 ** -0.5, 0.25, ((0, 8),), jnp.float32)
    return dict(field=field, basis_two=basis_two, basis_three=basis_three)


def reference(field, basis_two, basis_three):
    hp = lax.Precision.HIGHEST
    first = jnp.einsum("vacb,bs->vacs", field, basis_two, precision=hp)
    core = jnp.einsum("vacs,ct->avst", first, basis_three, precision=hp)
    projected = core.reshape(core.shape[0], -1)
    gram = jnp.dot(projected, projected.T, precision=hp, preferred_element_type=jnp.float32) / jnp.float32(K)
    return projected, gram
```

```python
import functools

import jax
import jax.numpy as jnp
from jax import lax
from jax.experimental import pallas as pl
from jax.experimental.pallas import tpu as pltpu
from jax.sharding import PartitionSpec as P

V = 4
R = 64
AXES = ("gx", "gy", "gz")
F32, BF16 = jnp.float32, jnp.bfloat16
STEP = 8


def split(x):
    hi = x.astype(BF16)
    return hi, (x - hi.astype(F32)).astype(BF16)


def dot(a, b, contract):
    return lax.dot_general(a, b, ((contract[:1], contract[1:]), ((), ())), preferred_element_type=F32)


def project_kernel(where, field, b2t, b3, mine, theirs, rows, w2, w3):
    @pl.when((pl.program_id(0) == 0) & (pl.program_id(1) == 0))
    def _():
        y, c = where[1], where[2]
        for other in range(2):
            for off in range(4):
                start = (lax.rem(y + off, 4) * 2 + lax.rem(c + other, 2)) * 8
                rows[pl.ds((other * 4 + off) * 8, 8), :] = b2t[pl.ds(pl.multiple_of(start, 8), 8), :]
        hi, lo = split(rows[...])
        w2[0:64, :] = hi
        w2[64:128, :] = lo
        wide = jnp.concatenate([b3[...]] * 4, axis=1)
        tall = jnp.concatenate([wide] * 4, axis=0)
        same = lax.broadcasted_iota(jnp.int32, (256, 256), 0) // 64 == lax.broadcasted_iota(jnp.int32, (256, 256), 1) // 64
        hi, lo = split(jnp.where(same, tall, 0.0))
        w3[0] = hi
        w3[1] = lo

    for q in range(STEP // 2):
        k = 2 * q
        x = jnp.concatenate([field[0, 0, k], field[0, 1, k], field[0, 0, k + 1], field[0, 1, k + 1]], axis=0)
        hi, lo = split(x)
        both = dot(w2[...], hi, (1, 1))
        first = both[:64] + both[64:] + dot(w2[0:64, :], lo, (1, 1))
        hi, lo = split(first)
        both = dot(jnp.concatenate([hi, lo], axis=0), w3[0], (1, 0))
        core = both[:64] + both[64:] + dot(hi, w3[1], (1, 0))
        lanes = slice(q * 256, (q + 1) * 256)
        mine[0, :, :, lanes] = core[:32].reshape(4, 8, 256)
        theirs[0, :, :, lanes] = core[32:].reshape(4, 8, 256)


def project(where, field, b2t, b3):
    steps = 32 // STEP
    part = jax.ShapeDtypeStruct((4, 4, 8, 4096), F32)
    part_spec = pl.BlockSpec((1, 4, 8, STEP * 128), lambda d, j, w: (d, 0, 0, j))
    return pl.pallas_call(
        project_kernel,
        out_shape=(part, part),
        grid_spec=pltpu.PrefetchScalarGridSpec(
            num_scalar_prefetch=1,
            grid=(4, steps),
            in_specs=[
                pl.BlockSpec((1, 2, STEP, 64, 256), lambda d, j, w: (lax.rem(w[0] + d, 4), 0, j, 0, 0)),
                pl.BlockSpec((64, 256), lambda d, j, w: (0, 0)),
                pl.BlockSpec((64, 64), lambda d, j, w: (0, 0)),
            ],
            out_specs=(part_spec, part_spec),
            scratch_shapes=[
                pltpu.VMEM((64, 256), F32),
                pltpu.VMEM((128, 256), BF16),
                pltpu.VMEM((2, 256, 256), BF16),
            ],
        ),
        compiler_params=pltpu.CompilerParams(vmem_limit_bytes=32 * 2**20),
        name="project",
    )(where, field, b2t, b3)


def add_kernel(where, *refs):
    for g in range(4):
        refs[8 + g][0] = refs[g][0, 0] + refs[4 + g][0, 0]


def add_groups(where, mine, received):
    def group(g):
        def index(h, w):
            swap = w[2]
            return (g + (h - g) * swap, h + (g - h) * swap, 0, 0)

        return pl.BlockSpec((1, 1, 8, 4096), index)

    return pl.pallas_call(
        add_kernel,
        out_shape=[jax.ShapeDtypeStruct((4, 8, 4096), F32)] * 4,
        grid_spec=pltpu.PrefetchScalarGridSpec(
            num_scalar_prefetch=1,
            grid=(4,),
            in_specs=[group(g) for g in range(4)] * 2,
            out_specs=[pl.BlockSpec((1, 8, 4096), lambda h, w: (h, 0, 0))] * 4,
        ),
        compiler_params=pltpu.CompilerParams(vmem_limit_bytes=32 * 2**20),
        name="add_cores",
    )(where, *([mine] * 4 + [received] * 4))


def sum_kernel(a, b, c, d, *outs):
    for h in range(4):
        outs[h][...] = (a[h] + b[h]) + (c[h] + d[h])


def sum_groups(parts):
    return pl.pallas_call(
        sum_kernel,
        out_shape=[jax.ShapeDtypeStruct((8, 4096), F32)] * 4,
        compiler_params=pltpu.CompilerParams(vmem_limit_bytes=32 * 2**20),
        name="sum_first_axis",
    )(*parts)


def finish_kernel(a, b, c, d, out, rows):
    total = (a[...] + b[...]) + (c[...] + d[...])
    for k in range(32):
        rows[:, k, :] = total[:, k * 128 : (k + 1) * 128]
    low = lax.broadcasted_iota(jnp.int32, (32, 128), 1) < 64
    for j in range(4):
        even, odd = rows[2 * j], rows[2 * j + 1]
        out[0:32, j * 128 : (j + 1) * 128] = jnp.where(low, even, pltpu.roll(odd, 64, 1))
        out[32:64, j * 128 : (j + 1) * 128] = jnp.where(low, pltpu.roll(even, 64, 1), odd)


def finish(parts):
    return pl.pallas_call(
        finish_kernel,
        out_shape=jax.ShapeDtypeStruct((64, 512), F32),
        scratch_shapes=[pltpu.VMEM((8, 32, 128), F32)],
        name="sum_second_axis",
    )(*parts)


def gram_kernel(z, a, b, c, d, out, cols):
    for off, ref in enumerate((a, b, c, d)):
        start = pl.multiple_of(lax.rem(z[0] + off, 4) * 64, 64)
        cols[pl.ds(start, 64), :] = ref[...]
    hi, lo = split(a[...])
    chi, clo = split(cols[...])
    both = dot(jnp.concatenate([hi, lo], axis=0), chi, (1, 1))
    out[...] = (both[:64] + both[64:] + dot(hi, clo, (1, 1))) * (1.0 / (V * R * R))


def gram_part(z, parts):
    return pl.pallas_call(
        gram_kernel,
        out_shape=jax.ShapeDtypeStruct((64, 256), F32),
        in_specs=[pl.BlockSpec(memory_space=pltpu.SMEM)] + [pl.BlockSpec(memory_space=pltpu.VMEM)] * 4,
        scratch_shapes=[pltpu.VMEM((256, 512), F32)],
        name="gram",
    )(z, *parts)


def pairs(target):
    out = []
    for z in range(4):
        for x in range(4):
            for y in range(4):
                for c in range(2):
                    tz, tx, ty, tc = target(z, x, y, c)
                    out.append((((z * 4 + x) * 4 + y) * 2 + c, (((tz % 4) * 4 + tx % 4) * 4 + ty % 4) * 2 + tc))
    return out


def send(x, target):
    return lax.ppermute(x, AXES, pairs(target))


def first_axis(off):
    return lambda z, x, y, c: (z, x + off * (1 - c), y + off * c, c)


def second_axis(off):
    return lambda z, x, y, c: (z, x + off * c, y + off * (1 - c), c)


def other_core(z, x, y, c):
    return (z, x, y, 1 - c)


def exchange(parts, axis):
    late = {off: send(parts[off], axis(off)) for off in (2, 1, 3)}
    return [parts[0], late[1], late[2], late[3]]


def total(x, axis):
    return sum(exchange([x] * 4, axis))


def body(field, basis_two, basis_three):
    z, x, gz = (lax.axis_index(a) for a in AXES)
    where = jnp.stack([x, gz // 2, gz % 2]).astype(jnp.int32)
    mine, theirs = project(where, field.reshape(4, 2, 32, 64, 256), basis_two.T, basis_three)
    groups = add_groups(where, mine, send(theirs, other_core))
    groups = sum_groups(exchange(groups, first_axis))
    projected = finish(exchange(groups, second_axis))
    rows = [projected] + [send(projected, lambda z, x, y, c, off=off: (z - off, x, y, c)) for off in (1, 2, 3)]
    part = gram_part(z.astype(jnp.int32).reshape(1), rows)
    part = part + send(part, other_core)
    gram = total(total(part, first_axis), second_axis)
    return (projected, gram)


def solution(mesh):
    placed = (P(None, "gx", "gz", "gy"), P("gy", None), P("gz", None))
    return jax.shard_map(
        body,
        mesh=mesh,
        in_specs=placed,
        out_specs=(P("gx", ("gy", "gz")), P("gx", None)),
        check_vma=False,
    )
```

```python
import functools

import jax
import jax.numpy as jnp
from jax import lax
from jax.experimental import pallas as pl
from jax.experimental.pallas import tpu as pltpu
from jax.sharding import PartitionSpec as P

V = 4
R = 64
AXES = ("gx", "gy", "gz")
F32, BF16 = jnp.float32, jnp.bfloat16
PARTS = ((0, 8), (8, 8))


def split(x):
    hi = x.astype(BF16)
    return hi, (x - hi.astype(F32)).astype(BF16)


def dot(a, b, contract):
    return lax.dot_general(a, b, ((contract[:1], contract[1:]), ((), ())), preferred_element_type=F32)


def project_kernel(begin, size, field, b2t_in, b3_in, mine, theirs, cells, b2t, b3, rows, w2, w3, sem, small_sem):
    x, gz = lax.axis_index("gy"), lax.axis_index("gz")
    small = [pltpu.make_async_copy(b2t_in, b2t, small_sem.at[0]), pltpu.make_async_copy(b3_in, b3, small_sem.at[1])]
    for copy in small:
        copy.start()

    def load(off):
        v = lax.rem(x + off, 4)
        return pltpu.make_async_copy(field.at[v, :, pl.ds(begin, size)], cells.at[off], sem.at[off])

    for off in range(4):
        load(off).start()
    for copy in small:
        copy.wait()

    for other in range(2):
        for off in range(4):
            start = (lax.rem(gz // 2 + off, 4) * 2 + lax.rem(gz + other, 2)) * 8
            rows[pl.ds((other * 4 + off) * 8, 8), :] = b2t[pl.ds(pl.multiple_of(start, 8), 8), :]
    hi, lo = split(rows[...].T)
    zero = jnp.zeros_like(hi)
    w2[0:256, :] = jnp.concatenate([hi, zero, lo, zero], axis=1)
    w2[256:512, :] = jnp.concatenate([zero, hi, zero, lo], axis=1)
    tall = jnp.concatenate([jnp.concatenate([b3[...]] * 2, axis=1)] * 2, axis=0)
    block = [lax.broadcasted_iota(jnp.int32, (128, 128), i) // 64 for i in range(2)]
    hi, lo = split(jnp.where(block[0] == block[1], tall, 0.0))
    w3[0:128, :] = hi
    w3[128:256, :] = hi
    w3[256:384, :] = lo

    def chunk(off, _):
        load(off).wait()
        quads = [
            jnp.concatenate([cells[off, i, m, 0], cells[off, i, m, 1]], axis=1) for m in range(size) for i in range(2)
        ]
        hi, lo = split(jnp.concatenate(quads, axis=0))
        both = dot(hi, w2[...], (1, 0))
        first = both[:, :128] + both[:, 128:] + dot(lo, w2[:, :128], (1, 0))
        for m in range(size):
            hi, lo = split(first[m * 128 : (m + 1) * 128].T)
            core = dot(jnp.concatenate([hi, lo, hi], axis=1), w3[...], (1, 0))
            for r in range(2):
                lanes = slice((2 * m + r) * 128, (2 * m + r + 1) * 128)
                mine[off, :, :, lanes] = core[r * 64 : r * 64 + 32].reshape(4, 8, 128)
                theirs[off, :, :, lanes] = core[r * 64 + 32 : r * 64 + 64].reshape(4, 8, 128)
        return 0

    lax.fori_loop(0, 4, chunk, 0)


def project(begin, size, field, b2t, b3):
    part = jax.ShapeDtypeStruct((4, 4, 8, size * 256), F32)
    return pl.pallas_call(
        functools.partial(project_kernel, begin, size),
        out_shape=(part, part),
        in_specs=[pl.BlockSpec(memory_space=pltpu.HBM)] * 3,
        out_specs=[pl.BlockSpec(memory_space=pltpu.VMEM)] * 2,
        scratch_shapes=[
            pltpu.VMEM((4, 2, size, 2, 64, 256), F32),
            pltpu.VMEM((64, 256), F32),
            pltpu.VMEM((64, 64), F32),
            pltpu.VMEM((64, 256), F32),
            pltpu.VMEM((512, 256), BF16),
            pltpu.VMEM((384, 128), BF16),
            pltpu.SemaphoreType.DMA((4,)),
            pltpu.SemaphoreType.DMA((2,)),
        ],
        compiler_params=pltpu.CompilerParams(vmem_limit_bytes=24 * 2**20),
        cost_estimate=pl.CostEstimate(flops=size * 10**9, bytes_accessed=size * 2**20, transcendentals=0),
        name=f"project_{begin}",
    )(*(pltpu.with_memory_space_constraint(a, pltpu.HBM) for a in (field, b2t, b3)))


def add_kernel(mine, received, *outs):
    core = lax.rem(lax.axis_index("gz"), 2)
    for g in range(4):
        for h in range(4):
            v, y = g + (h - g) * core, h + (g - h) * core
            outs[g][h] = mine[v, y] + received[v, y]


def add_groups(mine, received):
    return pl.pallas_call(
        add_kernel,
        out_shape=[jax.ShapeDtypeStruct(mine.shape[1:], F32)] * 4,
        compiler_params=pltpu.CompilerParams(vmem_limit_bytes=8 * 2**20),
        name="add_cores",
    )(mine, received)


def sum_kernel(*refs):
    ins, outs = refs[:-4], refs[-4:]
    lane = 0
    for p in range(0, len(ins), 4):
        a, b, c, d = ins[p : p + 4]
        lanes = slice(lane, lane + a.shape[-1])
        lane += a.shape[-1]
        for h in range(4):
            outs[h][:, lanes] = (a[h] + b[h]) + (c[h] + d[h])


def sum_groups(parts):
    return pl.pallas_call(
        sum_kernel,
        out_shape=[jax.ShapeDtypeStruct((8, 4096), F32)] * 4,
        compiler_params=pltpu.CompilerParams(vmem_limit_bytes=8 * 2**20),
        name="sum_first_axis",
    )(*[x for part in parts for x in part])


def finish_kernel(a, b, c, d, out):
    total = (a[...] + b[...]) + (c[...] + d[...])
    rows = total.reshape(8, 32, 128)
    low = lax.broadcasted_iota(jnp.int32, (32, 128), 1) < 64
    for j in range(4):
        even, odd = rows[2 * j], rows[2 * j + 1]
        out[0:32, j * 128 : (j + 1) * 128] = jnp.where(low, even, pltpu.roll(odd, 64, 1))
        out[32:64, j * 128 : (j + 1) * 128] = jnp.where(low, pltpu.roll(even, 64, 1), odd)


def finish(parts):
    return pl.pallas_call(
        finish_kernel,
        out_shape=jax.ShapeDtypeStruct((64, 512), F32),
        compiler_params=pltpu.CompilerParams(vmem_limit_bytes=8 * 2**20),
        name="sum_second_axis",
    )(*parts)


def gram_kernel(a, b, c, d, out, cols):
    z = lax.axis_index("gx")
    for off, ref in enumerate((a, b, c, d)):
        start = pl.multiple_of(lax.rem(z + off, 4) * 64, 64)
        cols[pl.ds(start, 64), :] = ref[...]
    hi, lo = split(a[...])
    chi, clo = split(cols[...])
    both = dot(jnp.concatenate([hi, lo], axis=0), chi, (1, 1))
    out[...] = (both[:64] + both[64:] + dot(hi, clo, (1, 1))) * (1.0 / (V * R * R))


def gram_part(parts):
    return pl.pallas_call(
        gram_kernel,
        out_shape=jax.ShapeDtypeStruct((64, 256), F32),
        scratch_shapes=[pltpu.VMEM((256, 512), F32)],
        compiler_params=pltpu.CompilerParams(vmem_limit_bytes=8 * 2**20),
        name="gram",
    )(*parts)


def pairs(target):
    out = []
    for z in range(4):
        for x in range(4):
            for y in range(4):
                for c in range(2):
                    tz, tx, ty, tc = target(z, x, y, c)
                    out.append((((z * 4 + x) * 4 + y) * 2 + c, (((tz % 4) * 4 + tx % 4) * 4 + ty % 4) * 2 + tc))
    return out


def send(x, target):
    return lax.ppermute(x, AXES, pairs(target))


def first_axis(off):
    return lambda z, x, y, c: (z, x + off * (1 - c), y + off * c, c)


def second_axis(off):
    return lambda z, x, y, c: (z, x + off * c, y + off * (1 - c), c)


def other_core(z, x, y, c):
    return (z, x, y, 1 - c)


def exchange(parts, axis):
    late = {off: send(parts[off], axis(off)) for off in (2, 1, 3)}
    return [parts[0], late[1], late[2], late[3]]


def total(x, axis):
    return sum(exchange([x] * 4, axis))


def body(field, basis_two, basis_three):
    field = field.reshape(4, 2, 16, 2, 64, 256)
    halves = [project(begin, size, field, basis_two.T, basis_three) for begin, size in PARTS]
    received = [send(theirs, other_core) for _, theirs in halves]
    groups = [add_groups(mine, part) for (mine, _), part in zip(halves, received)]
    groups = sum_groups([exchange(part, first_axis) for part in groups])
    projected = finish(exchange(groups, second_axis))
    rows = [projected] + [send(projected, lambda z, x, y, c, off=off: (z - off, x, y, c)) for off in (1, 2, 3)]
    part = gram_part(rows)
    part = part + send(part, other_core)
    gram = total(total(part, first_axis), second_axis)
    return (projected, gram)


def solution(mesh):
    placed = (P(None, "gx", "gz", "gy"), P("gy", None), P("gz", None))
    return jax.shard_map(
        body,
        mesh=mesh,
        in_specs=placed,
        out_specs=(P("gx", ("gy", "gz")), P("gx", None)),
        check_vma=False,
    )
```

```python
import functools

import jax
import jax.numpy as jnp
from jax import lax
from jax.experimental import pallas as pl
from jax.experimental.pallas import tpu as pltpu
from jax.sharding import PartitionSpec as P

V = 4
R = 64
OFFSETS = (0, 1, 3, 2)
AXES = ("gx", "gy", "gz")
F32, BF16 = jnp.float32, jnp.bfloat16
SIZES = (8, 8)


def split(x):
    hi = x.astype(BF16)
    return hi, (x - hi.astype(F32)).astype(BF16)


def dot(a, b, contract):
    return lax.dot_general(a, b, ((contract[:1], contract[1:]), ((), ())), preferred_element_type=F32)


def contract(cells, w2, w3, mine, theirs):
    size = cells.shape[1]
    quads = [
        jnp.concatenate([cells[i, m, 0], cells[i, m, 1]], axis=1) for m in range(size) for i in range(2)
    ]
    hi, lo = split(jnp.concatenate(quads, axis=0))
    both = dot(hi, w2[...], (1, 0))
    first = both[:, :128] + both[:, 128:] + dot(lo, w2[:, :128], (1, 0))
    for m in range(size):
        hi, lo = split(first[m * 128 : (m + 1) * 128].T)
        core = dot(jnp.concatenate([hi, lo, hi], axis=1), w3[...], (1, 0))
        for r in range(2):
            lanes = slice((2 * m + r) * 128, (2 * m + r + 1) * 128)
            mine[:, :, lanes] = core[r * 64 : r * 64 + 32].reshape(4, 8, 128)
            theirs[:, :, lanes] = core[r * 64 + 32 : r * 64 + 64].reshape(4, 8, 128)


def first_part_kernel(field, b2t_in, b3_in, mine, theirs, later, w2, w3, cells, b2t, b3, rows, sem, small_sem):
    x, gz = lax.axis_index("gy"), lax.axis_index("gz")
    small = [pltpu.make_async_copy(b2t_in, b2t, small_sem.at[0]), pltpu.make_async_copy(b3_in, b3, small_sem.at[1])]
    for copy in small:
        copy.start()

    def load(n):
        part, off = n // 4, n % 4
        cut = pl.ds(part * SIZES[0], SIZES[part])
        to = later if part else cells
        return pltpu.make_async_copy(field.at[lax.rem(x + off, 4), :, cut], to.at[off], sem.at[n])

    load(0).start()
    for copy in small:
        copy.wait()

    for other in range(2):
        for off in range(4):
            start = (lax.rem(gz // 2 + off, 4) * 2 + lax.rem(gz + other, 2)) * 8
            rows[pl.ds((other * 4 + off) * 8, 8), :] = b2t[pl.ds(pl.multiple_of(start, 8), 8), :]
    hi, lo = split(rows[...].T)
    zero = jnp.zeros_like(hi)
    w2[0:256, :] = jnp.concatenate([hi, zero, lo, zero], axis=1)
    w2[256:512, :] = jnp.concatenate([zero, hi, zero, lo], axis=1)
    tall = jnp.concatenate([jnp.concatenate([b3[...]] * 2, axis=1)] * 2, axis=0)
    block = [lax.broadcasted_iota(jnp.int32, (128, 128), i) // 64 for i in range(2)]
    hi, lo = split(jnp.where(block[0] == block[1], tall, 0.0))
    w3[0:128, :] = hi
    w3[128:256, :] = hi
    w3[256:384, :] = lo

    load(1).start()
    for off, ahead in enumerate(((2,), (3, 4), (5, 6), ())):
        load(off).wait()
        for n in ahead:
            load(n).start()
        contract(cells.at[off], w2, w3, mine.at[off], theirs.at[off])
    for n in range(4, 7):
        load(n).wait()


def second_part_kernel(field, early, w2, w3, mine, theirs, late, sem):
    x = lax.axis_index("gy")

    def load():
        cut = pl.ds(SIZES[0], SIZES[1])
        return pltpu.make_async_copy(field.at[lax.rem(x + 3, 4), :, cut], late, sem)

    load().start()
    for off in range(4):
        if off == 3:
            load().wait()
        contract(early.at[off] if off < 3 else late, w2, w3, mine.at[off], theirs.at[off])


def project(field, b2t, b3):
    parts = [jax.ShapeDtypeStruct((4, 4, 8, size * 256), F32) for size in SIZES]
    cells = [(4, 2, size, 2, 64, 256) for size in SIZES]
    costs = [pl.CostEstimate(flops=size * 10**9, bytes_accessed=size * 2**20, transcendentals=0) for size in SIZES]
    params = pltpu.CompilerParams(vmem_limit_bytes=26 * 2**20)
    vmem = pl.BlockSpec(memory_space=pltpu.VMEM)
    field, b2t, b3 = (pltpu.with_memory_space_constraint(a, pltpu.HBM) for a in (field, b2t, b3))
    mine, theirs, later, w2, w3 = pl.pallas_call(
        first_part_kernel,
        out_shape=(
            parts[0],
            parts[0],
            jax.ShapeDtypeStruct((3, *cells[1][1:]), F32),
            jax.ShapeDtypeStruct((512, 256), BF16),
            jax.ShapeDtypeStruct((384, 128), BF16),
        ),
        in_specs=[pl.BlockSpec(memory_space=pltpu.HBM)] * 3,
        out_specs=[vmem] * 5,
        scratch_shapes=[
            pltpu.VMEM(cells[0], F32),
            pltpu.VMEM((64, 256), F32),
            pltpu.VMEM((64, 64), F32),
            pltpu.VMEM((64, 256), F32),
            pltpu.SemaphoreType.DMA((7,)),
            pltpu.SemaphoreType.DMA((2,)),
        ],
        compiler_params=params,
        cost_estimate=costs[0],
        name="project_first_part",
    )(field, b2t, b3)
    second = pl.pallas_call(
        second_part_kernel,
        out_shape=(parts[1], parts[1]),
        in_specs=[pl.BlockSpec(memory_space=pltpu.HBM)] + [vmem] * 3,
        out_specs=[vmem] * 2,
        scratch_shapes=[pltpu.VMEM(cells[1][1:], F32), pltpu.SemaphoreType.DMA],
        compiler_params=params,
        cost_estimate=costs[1],
        name="project_second_part",
    )(field, later, w2, w3)
    return (mine, theirs), second


def add_kernel(mine, received, *rest):
    outs = rest[-4:]
    core = lax.rem(lax.axis_index("gz"), 2)
    for g in range(4):
        for h in range(4):
            v, y = g + (h - g) * core, h + (g - h) * core
            outs[g][h] = mine[v, y] + received[v, y]


def add_groups(mine, received, after):
    vmem = pl.BlockSpec(memory_space=pltpu.VMEM)
    return pl.pallas_call(
        add_kernel,
        in_specs=[vmem] * 2 + [pl.BlockSpec(memory_space=pl.ANY)] * len(after),
        out_shape=[jax.ShapeDtypeStruct(mine.shape[1:], F32)] * 4,
        compiler_params=pltpu.CompilerParams(vmem_limit_bytes=8 * 2**20),
        name="add_cores",
    )(mine, received, *after)


def sum_kernel(*refs):
    ins, outs = refs[:-4], refs[-4:]
    lane = 0
    for p in range(0, len(ins), 4):
        a, b, c, d = ins[p : p + 4]
        lanes = slice(lane, lane + a.shape[-1])
        lane += a.shape[-1]
        for h in range(4):
            outs[h][:, lanes] = (a[h] + b[h]) + (c[h] + d[h])


def sum_groups(parts):
    return pl.pallas_call(
        sum_kernel,
        out_shape=[jax.ShapeDtypeStruct((8, 4096), F32)] * 4,
        compiler_params=pltpu.CompilerParams(vmem_limit_bytes=8 * 2**20),
        name="sum_first_axis",
    )(*[x for part in parts for x in part])


def finish_kernel(a, b, c, d, out):
    total = (a[...] + b[...]) + (c[...] + d[...])
    pairs = total.shape[1] // 128
    rows = total.reshape(8, pairs, 128)
    low = lax.broadcasted_iota(jnp.int32, (pairs, 128), 1) < 64
    for j in range(4):
        even, odd = rows[2 * j], rows[2 * j + 1]
        lanes = slice(j * 128, (j + 1) * 128)
        out[0:pairs, lanes] = jnp.where(low, even, pltpu.roll(odd, 64, 1))
        out[pairs : 2 * pairs, lanes] = jnp.where(low, pltpu.roll(even, 64, 1), odd)


def finish(parts):
    return pl.pallas_call(
        finish_kernel,
        out_shape=jax.ShapeDtypeStruct((parts[0].shape[1] // 64, 512), F32),
        compiler_params=pltpu.CompilerParams(vmem_limit_bytes=8 * 2**20),
        name="sum_second_axis",
    )(*parts)


def copy_kernel(x, out):
    out[...] = x[...]


def copy(x):
    return pl.pallas_call(
        copy_kernel,
        out_shape=jax.ShapeDtypeStruct(x.shape, x.dtype),
        compiler_params=pltpu.CompilerParams(vmem_limit_bytes=8 * 2**20),
        name="copy",
    )(x)


def gram_kernel(a, b, c, d, out, cols):
    z = lax.axis_index("gx")
    for off, ref in zip(OFFSETS, (a, b, c, d)):
        start = pl.multiple_of(lax.rem(z + off, 4) * 64, 64)
        cols[pl.ds(start, 64), :] = ref[...]
    hi, lo = split(a[...])
    chi, clo = split(cols[...])
    both = dot(jnp.concatenate([hi, lo], axis=0), chi, (1, 1))
    out[...] = (both[:64] + both[64:] + dot(hi, clo, (1, 1))) * (1.0 / (V * R * R))


def gram_part(parts):
    return pl.pallas_call(
        gram_kernel,
        out_shape=jax.ShapeDtypeStruct((64, 256), F32),
        scratch_shapes=[pltpu.VMEM((256, 512), F32)],
        compiler_params=pltpu.CompilerParams(vmem_limit_bytes=8 * 2**20),
        name="gram",
    )(*parts)


def pairs(target):
    out = []
    for z in range(4):
        for x in range(4):
            for y in range(4):
                for c in range(2):
                    tz, tx, ty, tc = target(z, x, y, c)
                    out.append((((z * 4 + x) * 4 + y) * 2 + c, (((tz % 4) * 4 + tx % 4) * 4 + ty % 4) * 2 + tc))
    return out


def send(x, target):
    return lax.ppermute(x, AXES, pairs(target))


def first_axis(off):
    return lambda z, x, y, c: (z, x + off * (1 - c), y + off * c, c)


def second_axis(off):
    return lambda z, x, y, c: (z, x + off * c, y + off * (1 - c), c)


def other_core(z, x, y, c):
    return (z, x, y, 1 - c)


def exchange(parts, axis):
    return [parts[0]] + [send(parts[off], axis(off)) for off in (2, 1, 3)]


def total(x, axis):
    return sum([x] + [send(x, axis(off)) for off in (1, 3, 2)])


def body(field, basis_two, basis_three):
    field = field.reshape(4, 2, 16, 2, 64, 256)
    halves = project(field, basis_two.T, basis_three)
    received = [send(theirs, other_core) for _, theirs in halves]
    groups = []
    for (mine, _), part in zip(halves, received):
        groups.append(add_groups(mine, part, groups[-1][:1] if groups else []))
    groups = sum_groups([exchange(part, first_axis) for part in groups])
    rows = finish(exchange(groups, second_axis))
    gathered = [rows] + [send(rows, lambda z, x, y, c, off=off: (z - off, x, y, c)) for off in OFFSETS[1:]]
    gram = total(total(gram_part(gathered), first_axis), second_axis)
    return (copy(rows), gram + send(gram, other_core))


def solution(mesh):
    placed = (P(None, "gx", "gz", "gy"), P("gy", None), P("gz", None))
    return jax.shard_map(
        body,
        mesh=mesh,
        in_specs=placed,
        out_specs=(P("gx", ("gy", "gz")), P("gx", None)),
        check_vma=False,
    )
```

```python
import functools

import jax
import jax.numpy as jnp
from jax import lax
from jax.experimental import pallas as pl
from jax.experimental.pallas import tpu as pltpu
from jax.sharding import PartitionSpec as P

V = 4
R = 64
OFFSETS = (0, 2, 1, 3)
FIRST = ((2, 1, 3), (2, 1, 3))
SECOND = (1, 3, 2)
AXES = ("gx", "gy", "gz")
F32, BF16 = jnp.float32, jnp.bfloat16
SIZES = (8, 8)


def split(x):
    hi = x.astype(BF16)
    return hi, (x - hi.astype(F32)).astype(BF16)


def dot(a, b, contract):
    return lax.dot_general(a, b, ((contract[:1], contract[1:]), ((), ())), preferred_element_type=F32)


def contract(cells, w2, w3, mine, theirs):
    size = cells.shape[1]
    quads = [
        jnp.concatenate([cells[i, m, 0], cells[i, m, 1]], axis=1) for m in range(size) for i in range(2)
    ]
    hi, lo = split(jnp.concatenate(quads, axis=0))
    both = dot(hi, w2[...], (1, 0))
    first = both[:, :128] + both[:, 128:] + dot(lo, w2[:, :128], (1, 0))
    for m in range(size):
        hi, lo = split(first[m * 128 : (m + 1) * 128].T)
        core = dot(jnp.concatenate([hi, lo, hi], axis=1), w3[...], (1, 0))
        for r in range(2):
            lanes = slice((2 * m + r) * 128, (2 * m + r + 1) * 128)
            mine[:, :, lanes] = core[r * 64 : r * 64 + 32].reshape(4, 8, 128)
            theirs[:, :, lanes] = core[r * 64 + 32 : r * 64 + 64].reshape(4, 8, 128)


def first_part_kernel(field, b2t_in, b3_in, mine, theirs, later, w2, w3, cells, b2t, b3, rows, sem, small_sem):
    x, gz = lax.axis_index("gy"), lax.axis_index("gz")
    small = [pltpu.make_async_copy(b2t_in, b2t, small_sem.at[0]), pltpu.make_async_copy(b3_in, b3, small_sem.at[1])]
    for copy in small:
        copy.start()

    def load(n):
        part, off = n // 4, n % 4
        cut = pl.ds(part * SIZES[0], SIZES[part])
        to = later if part else cells
        return pltpu.make_async_copy(field.at[lax.rem(x + off, 4), :, cut], to.at[off], sem.at[n])

    load(0).start()
    for copy in small:
        copy.wait()

    for other in range(2):
        for off in range(4):
            start = (lax.rem(gz // 2 + off, 4) * 2 + lax.rem(gz + other, 2)) * 8
            rows[pl.ds((other * 4 + off) * 8, 8), :] = b2t[pl.ds(pl.multiple_of(start, 8), 8), :]
    hi, lo = split(rows[...].T)
    zero = jnp.zeros_like(hi)
    w2[0:256, :] = jnp.concatenate([hi, zero, lo, zero], axis=1)
    w2[256:512, :] = jnp.concatenate([zero, hi, zero, lo], axis=1)
    tall = jnp.concatenate([jnp.concatenate([b3[...]] * 2, axis=1)] * 2, axis=0)
    block = [lax.broadcasted_iota(jnp.int32, (128, 128), i) // 64 for i in range(2)]
    hi, lo = split(jnp.where(block[0] == block[1], tall, 0.0))
    w3[0:128, :] = hi
    w3[128:256, :] = hi
    w3[256:384, :] = lo

    load(1).start()
    for off, ahead in enumerate(((2,), (3, 4), (5, 6), ())):
        load(off).wait()
        for n in ahead:
            load(n).start()
        contract(cells.at[off], w2, w3, mine.at[off], theirs.at[off])
    for n in range(4, 7):
        load(n).wait()


def second_part_kernel(field, early, w2, w3, mine, theirs, late, sem):
    x = lax.axis_index("gy")

    def load():
        cut = pl.ds(SIZES[0], SIZES[1])
        return pltpu.make_async_copy(field.at[lax.rem(x + 3, 4), :, cut], late, sem)

    load().start()
    for off in range(4):
        if off == 3:
            load().wait()
        contract(early.at[off] if off < 3 else late, w2, w3, mine.at[off], theirs.at[off])


def project(field, b2t, b3):
    parts = [jax.ShapeDtypeStruct((4, 4, 8, size * 256), F32) for size in SIZES]
    cells = [(4, 2, size, 2, 64, 256) for size in SIZES]
    costs = [pl.CostEstimate(flops=size * 10**9, bytes_accessed=size * 2**20, transcendentals=0) for size in SIZES]
    params = pltpu.CompilerParams(vmem_limit_bytes=26 * 2**20)
    vmem = pl.BlockSpec(memory_space=pltpu.VMEM)
    field, b2t, b3 = (pltpu.with_memory_space_constraint(a, pltpu.HBM) for a in (field, b2t, b3))
    mine, theirs, later, w2, w3 = pl.pallas_call(
        first_part_kernel,
        out_shape=(
            parts[0],
            parts[0],
            jax.ShapeDtypeStruct((3, *cells[1][1:]), F32),
            jax.ShapeDtypeStruct((512, 256), BF16),
            jax.ShapeDtypeStruct((384, 128), BF16),
        ),
        in_specs=[pl.BlockSpec(memory_space=pltpu.HBM)] * 3,
        out_specs=[vmem] * 5,
        scratch_shapes=[
            pltpu.VMEM(cells[0], F32),
            pltpu.VMEM((64, 256), F32),
            pltpu.VMEM((64, 64), F32),
            pltpu.VMEM((64, 256), F32),
            pltpu.SemaphoreType.DMA((7,)),
            pltpu.SemaphoreType.DMA((2,)),
        ],
        compiler_params=params,
        cost_estimate=costs[0],
        name="project_first_part",
    )(field, b2t, b3)
    second = pl.pallas_call(
        second_part_kernel,
        out_shape=(parts[1], parts[1]),
        in_specs=[pl.BlockSpec(memory_space=pltpu.HBM)] + [vmem] * 3,
        out_specs=[vmem] * 2,
        scratch_shapes=[pltpu.VMEM(cells[1][1:], F32), pltpu.SemaphoreType.DMA],
        compiler_params=params,
        cost_estimate=costs[1],
        name="project_second_part",
    )(field, later, w2, w3)
    return (mine, theirs), second


def add_kernel(mine, received, *rest):
    outs = rest[-4:]
    core = lax.rem(lax.axis_index("gz"), 2)
    for g in range(4):
        for h in range(4):
            v, y = g + (h - g) * core, h + (g - h) * core
            outs[g][h] = mine[v, y] + received[v, y]


def add_groups(mine, received, after):
    vmem = pl.BlockSpec(memory_space=pltpu.VMEM)
    return pl.pallas_call(
        add_kernel,
        in_specs=[vmem] * 2 + [pl.BlockSpec(memory_space=pl.ANY)] * len(after),
        out_shape=[jax.ShapeDtypeStruct(mine.shape[1:], F32)] * 4,
        compiler_params=pltpu.CompilerParams(vmem_limit_bytes=8 * 2**20),
        name="add_cores",
    )(mine, received, *after)


def sum_kernel(*refs):
    ins, outs = refs[:-4], refs[-4:]
    lane = 0
    for p in range(0, len(ins), 4):
        a, b, c, d = ins[p : p + 4]
        lanes = slice(lane, lane + a.shape[-1])
        lane += a.shape[-1]
        for h in range(4):
            outs[h][:, lanes] = (a[h] + b[h]) + (c[h] + d[h])


def sum_groups(parts):
    return pl.pallas_call(
        sum_kernel,
        out_shape=[jax.ShapeDtypeStruct((8, 4096), F32)] * 4,
        compiler_params=pltpu.CompilerParams(vmem_limit_bytes=8 * 2**20),
        name="sum_first_axis",
    )(*[x for part in parts for x in part])


def finish_kernel(a, b, c, d, out):
    total = (a[...] + b[...]) + (c[...] + d[...])
    pairs = total.shape[1] // 128
    rows = total.reshape(8, pairs, 128)
    low = lax.broadcasted_iota(jnp.int32, (pairs, 128), 1) < 64
    for j in range(4):
        even, odd = rows[2 * j], rows[2 * j + 1]
        lanes = slice(j * 128, (j + 1) * 128)
        out[0:pairs, lanes] = jnp.where(low, even, pltpu.roll(odd, 64, 1))
        out[pairs : 2 * pairs, lanes] = jnp.where(low, pltpu.roll(even, 64, 1), odd)


def finish(parts):
    return pl.pallas_call(
        finish_kernel,
        out_shape=jax.ShapeDtypeStruct((parts[0].shape[1] // 64, 512), F32),
        compiler_params=pltpu.CompilerParams(vmem_limit_bytes=8 * 2**20),
        name="sum_second_axis",
    )(*parts)


def copy_kernel(x, out):
    out[...] = x[...]


def copy(x):
    return pl.pallas_call(
        copy_kernel,
        out_shape=jax.ShapeDtypeStruct(x.shape, x.dtype),
        compiler_params=pltpu.CompilerParams(vmem_limit_bytes=8 * 2**20),
        name="copy",
    )(x)


def gram_kernel(a, b, c, d, out, cols):
    z = lax.axis_index("gx")
    for off, ref in zip(OFFSETS, (a, b, c, d)):
        start = pl.multiple_of(lax.rem(z + off, 4) * 64, 64)
        cols[pl.ds(start, 64), :] = ref[...]
    hi, lo = split(a[...])
    chi, clo = split(cols[...])
    both = dot(jnp.concatenate([hi, lo], axis=0), chi, (1, 1))
    out[...] = (both[:64] + both[64:] + dot(hi, clo, (1, 1))) * (1.0 / (V * R * R))


def gram_part(parts):
    return pl.pallas_call(
        gram_kernel,
        out_shape=jax.ShapeDtypeStruct((64, 256), F32),
        scratch_shapes=[pltpu.VMEM((256, 512), F32)],
        compiler_params=pltpu.CompilerParams(vmem_limit_bytes=8 * 2**20),
        name="gram",
    )(*parts)


def pairs(target):
    out = []
    for z in range(4):
        for x in range(4):
            for y in range(4):
                for c in range(2):
                    tz, tx, ty, tc = target(z, x, y, c)
                    out.append((((z * 4 + x) * 4 + y) * 2 + c, (((tz % 4) * 4 + tx % 4) * 4 + ty % 4) * 2 + tc))
    return out


def send(x, target):
    return lax.ppermute(x, AXES, pairs(target))


def first_axis(off):
    return lambda z, x, y, c: (z, x + off * (1 - c), y + off * c, c)


def second_axis(off):
    return lambda z, x, y, c: (z, x + off * c, y + off * (1 - c), c)


def other_core(z, x, y, c):
    return (z, x, y, 1 - c)


def exchange(parts, axis, order):
    return [parts[0]] + [send(parts[off], axis(off)) for off in order]


def add_halves_kernel(*refs):
    ins, (out, half) = refs[:-2], refs[-2:]
    total = sum(x[...] for x in ins[1:]) + ins[0][...]
    rows = half.shape[0]
    out[...] = total
    half[...] = jnp.where(lax.rem(lax.axis_index("gz"), 2) == 0, total[:rows], total[rows:])


def add_halves(*parts):
    rows, lanes = parts[0].shape
    return pl.pallas_call(
        add_halves_kernel,
        out_shape=[jax.ShapeDtypeStruct((rows, lanes), F32), jax.ShapeDtypeStruct((rows // 2, lanes), F32)],
        compiler_params=pltpu.CompilerParams(vmem_limit_bytes=8 * 2**20),
        name="add_halves",
    )(*parts)


def hear_kernel(whole, half, out):
    rows = half.shape[0]
    out[...] = whole[...]
    mine = pl.ds(pl.multiple_of(lax.rem(lax.axis_index("gz"), 2) * rows, rows), rows)
    out[mine, :] = out[mine, :] + half[...]


def hear(whole, half):
    return pl.pallas_call(
        hear_kernel,
        out_shape=jax.ShapeDtypeStruct(whole.shape, F32),
        compiler_params=pltpu.CompilerParams(vmem_limit_bytes=8 * 2**20),
        name="hear",
    )(whole, half)


def plane_total(part):
    terms = (part, send(part, other_core))
    for along_x in (1, 0):

        def whole(z, x, y, c):
            step = 2 - c
            return (z, x + step * along_x, y + step * (1 - along_x), c)

        def shared(z, x, y, c):
            return (z, x + 3 * along_x, y + 3 * (1 - along_x), c)

        part, half = add_halves(*terms)
        heard = hear(send(part, whole), send(half, shared))
        terms = (part, heard, send(heard, other_core))
    return sum(terms)


def body(field, basis_two, basis_three):
    field = field.reshape(4, 2, 16, 2, 64, 256)
    halves = project(field, basis_two.T, basis_three)
    received = [send(theirs, other_core) for _, theirs in halves]
    groups = []
    for (mine, _), part in zip(halves, received):
        groups.append(add_groups(mine, part, groups[-1][:1] if groups else []))
    groups = sum_groups([exchange(part, first_axis, order) for part, order in zip(groups, FIRST)])
    rows = finish(exchange(groups, second_axis, SECOND))
    gathered = [rows] + [send(rows, lambda z, x, y, c, off=off: (z - off, x, y, c)) for off in OFFSETS[1:]]
    return (copy(rows), plane_total(gram_part(gathered)))


def solution(mesh):
    placed = (P(None, "gx", "gz", "gy"), P("gy", None), P("gz", None))
    return jax.shard_map(
        body,
        mesh=mesh,
        in_specs=placed,
        out_specs=(P("gx", ("gy", "gz")), P("gx", None)),
        check_vma=False,
    )
```

```python
import functools

import jax
import jax.numpy as jnp
from jax import lax
from jax.experimental import pallas as pl
from jax.experimental.pallas import tpu as pltpu
from jax.sharding import PartitionSpec as P

V = 4
R = 64
OFFSETS = (0, 2, 1, 3)
FIRST = ((1, 3, 2), (1, 3, 2))
SECOND = (1, 3, 2)
AXES = ("gx", "gy", "gz")
F32, BF16 = jnp.float32, jnp.bfloat16
SIZES = (8, 8)


def split(x):
    hi = x.astype(BF16)
    return hi, (x - hi.astype(F32)).astype(BF16)


def dot(a, b, contract):
    return lax.dot_general(a, b, ((contract[:1], contract[1:]), ((), ())), preferred_element_type=F32)


def contract(cells, w2, w3, mine, theirs):
    size = cells.shape[1]
    quads = [
        jnp.concatenate([cells[i, m, 0], cells[i, m, 1]], axis=1) for m in range(size) for i in range(2)
    ]
    hi, lo = split(jnp.concatenate(quads, axis=0))
    both = dot(hi, w2[...], (1, 0))
    first = both[:, :128] + both[:, 128:] + dot(lo, w2[:, :128], (1, 0))
    for m in range(size):
        hi, lo = split(first[m * 128 : (m + 1) * 128].T)
        core = dot(jnp.concatenate([hi, lo, hi], axis=1), w3[...], (1, 0))
        for r in range(2):
            lanes = slice((2 * m + r) * 128, (2 * m + r + 1) * 128)
            mine[:, :, lanes] = core[r * 64 : r * 64 + 32].reshape(4, 8, 128)
            theirs[:, :, lanes] = core[r * 64 + 32 : r * 64 + 64].reshape(4, 8, 128)


def first_part_kernel(field, b2t_in, b3_in, mine, theirs, later, w2, w3, cells, b2t, b3, rows, sem, small_sem):
    x, gz = lax.axis_index("gy"), lax.axis_index("gz")
    small = [pltpu.make_async_copy(b2t_in, b2t, small_sem.at[0]), pltpu.make_async_copy(b3_in, b3, small_sem.at[1])]
    for copy in small:
        copy.start()

    def load(n):
        part, off = n // 4, n % 4
        cut = pl.ds(part * SIZES[0], SIZES[part])
        to = later if part else cells
        return pltpu.make_async_copy(field.at[lax.rem(x + off, 4), :, cut], to.at[off], sem.at[n])

    load(0).start()
    for copy in small:
        copy.wait()

    for other in range(2):
        for off in range(4):
            start = (lax.rem(gz // 2 + off, 4) * 2 + lax.rem(gz + other, 2)) * 8
            rows[pl.ds((other * 4 + off) * 8, 8), :] = b2t[pl.ds(pl.multiple_of(start, 8), 8), :]
    hi, lo = split(rows[...].T)
    zero = jnp.zeros_like(hi)
    w2[0:256, :] = jnp.concatenate([hi, zero, lo, zero], axis=1)
    w2[256:512, :] = jnp.concatenate([zero, hi, zero, lo], axis=1)
    tall = jnp.concatenate([jnp.concatenate([b3[...]] * 2, axis=1)] * 2, axis=0)
    block = [lax.broadcasted_iota(jnp.int32, (128, 128), i) // 64 for i in range(2)]
    hi, lo = split(jnp.where(block[0] == block[1], tall, 0.0))
    w3[0:128, :] = hi
    w3[128:256, :] = hi
    w3[256:384, :] = lo

    load(1).start()
    for off, ahead in enumerate(((2, 3), (4, 5), (6,), ())):
        load(off).wait()
        for n in ahead:
            load(n).start()
        contract(cells.at[off], w2, w3, mine.at[off], theirs.at[off])
    for n in range(4, 7):
        load(n).wait()


def second_part_kernel(field, early, w2, w3, mine, theirs, late, sem):
    x = lax.axis_index("gy")

    def load():
        cut = pl.ds(SIZES[0], SIZES[1])
        return pltpu.make_async_copy(field.at[lax.rem(x + 3, 4), :, cut], late, sem)

    load().start()
    for off in range(4):
        if off == 3:
            load().wait()
        contract(early.at[off] if off < 3 else late, w2, w3, mine.at[off], theirs.at[off])


def project(field, b2t, b3):
    parts = [jax.ShapeDtypeStruct((4, 4, 8, size * 256), F32) for size in SIZES]
    cells = [(4, 2, size, 2, 64, 256) for size in SIZES]
    costs = [pl.CostEstimate(flops=size * 10**9, bytes_accessed=size * 2**20, transcendentals=0) for size in SIZES]
    params = pltpu.CompilerParams(vmem_limit_bytes=26 * 2**20)
    vmem = pl.BlockSpec(memory_space=pltpu.VMEM)
    field, b2t, b3 = (pltpu.with_memory_space_constraint(a, pltpu.HBM) for a in (field, b2t, b3))
    mine, theirs, later, w2, w3 = pl.pallas_call(
        first_part_kernel,
        out_shape=(
            parts[0],
            parts[0],
            jax.ShapeDtypeStruct((3, *cells[1][1:]), F32),
            jax.ShapeDtypeStruct((512, 256), BF16),
            jax.ShapeDtypeStruct((384, 128), BF16),
        ),
        in_specs=[pl.BlockSpec(memory_space=pltpu.HBM)] * 3,
        out_specs=[vmem] * 5,
        scratch_shapes=[
            pltpu.VMEM(cells[0], F32),
            pltpu.VMEM((64, 256), F32),
            pltpu.VMEM((64, 64), F32),
            pltpu.VMEM((64, 256), F32),
            pltpu.SemaphoreType.DMA((7,)),
            pltpu.SemaphoreType.DMA((2,)),
        ],
        compiler_params=params,
        cost_estimate=costs[0],
        name="project_first_part",
    )(field, b2t, b3)
    second = pl.pallas_call(
        second_part_kernel,
        out_shape=(parts[1], parts[1]),
        in_specs=[pl.BlockSpec(memory_space=pltpu.HBM)] + [vmem] * 3,
        out_specs=[vmem] * 2,
        scratch_shapes=[pltpu.VMEM(cells[1][1:], F32), pltpu.SemaphoreType.DMA],
        compiler_params=params,
        cost_estimate=costs[1],
        name="project_second_part",
    )(field, later, w2, w3)
    return (mine, theirs), second


def add_kernel(mine, received, *rest):
    outs = rest[-4:]
    core = lax.rem(lax.axis_index("gz"), 2)
    for g in range(4):
        for h in range(4):
            v, y = g + (h - g) * core, h + (g - h) * core
            outs[g][h] = mine[v, y] + received[v, y]


def add_groups(mine, received, after):
    vmem = pl.BlockSpec(memory_space=pltpu.VMEM)
    return pl.pallas_call(
        add_kernel,
        in_specs=[vmem] * 2 + [pl.BlockSpec(memory_space=pl.ANY)] * len(after),
        out_shape=[jax.ShapeDtypeStruct(mine.shape[1:], F32)] * 4,
        compiler_params=pltpu.CompilerParams(vmem_limit_bytes=8 * 2**20),
        name="add_cores",
    )(mine, received, *after)


def sum_kernel(*refs):
    ins, outs = refs[:-4], refs[-4:]
    lane = 0
    for p in range(0, len(ins), 4):
        a, b, c, d = ins[p : p + 4]
        lanes = slice(lane, lane + a.shape[-1])
        lane += a.shape[-1]
        for h in range(4):
            outs[h][:, lanes] = (a[h] + b[h]) + (c[h] + d[h])


def sum_groups(parts):
    return pl.pallas_call(
        sum_kernel,
        out_shape=[jax.ShapeDtypeStruct((8, 4096), F32)] * 4,
        compiler_params=pltpu.CompilerParams(vmem_limit_bytes=8 * 2**20),
        name="sum_first_axis",
    )(*[x for part in parts for x in part])


def finish_kernel(a, b, c, d, out):
    total = (a[...] + b[...]) + (c[...] + d[...])
    pairs = total.shape[1] // 128
    rows = total.reshape(8, pairs, 128)
    low = lax.broadcasted_iota(jnp.int32, (pairs, 128), 1) < 64
    for j in range(4):
        even, odd = rows[2 * j], rows[2 * j + 1]
        lanes = slice(j * 128, (j + 1) * 128)
        out[0:pairs, lanes] = jnp.where(low, even, pltpu.roll(odd, 64, 1))
        out[pairs : 2 * pairs, lanes] = jnp.where(low, pltpu.roll(even, 64, 1), odd)


def finish(parts):
    return pl.pallas_call(
        finish_kernel,
        out_shape=jax.ShapeDtypeStruct((parts[0].shape[1] // 64, 512), F32),
        compiler_params=pltpu.CompilerParams(vmem_limit_bytes=8 * 2**20),
        name="sum_second_axis",
    )(*parts)


def copy_kernel(x, out):
    out[...] = x[...]


def copy(x):
    return pl.pallas_call(
        copy_kernel,
        out_shape=jax.ShapeDtypeStruct(x.shape, x.dtype),
        compiler_params=pltpu.CompilerParams(vmem_limit_bytes=8 * 2**20),
        name="copy",
    )(x)


def gram_kernel(a, b, c, d, out, cols):
    z = lax.axis_index("gx")
    for off, ref in zip(OFFSETS, (a, b, c, d)):
        start = pl.multiple_of(lax.rem(z + off, 4) * 64, 64)
        cols[pl.ds(start, 64), :] = ref[...]
    hi, lo = split(a[...])
    chi, clo = split(cols[...])
    both = dot(jnp.concatenate([hi, lo], axis=0), chi, (1, 1))
    out[...] = (both[:64] + both[64:] + dot(hi, clo, (1, 1))) * (1.0 / (V * R * R))


def gram_part(parts):
    return pl.pallas_call(
        gram_kernel,
        out_shape=jax.ShapeDtypeStruct((64, 256), F32),
        scratch_shapes=[pltpu.VMEM((256, 512), F32)],
        compiler_params=pltpu.CompilerParams(vmem_limit_bytes=8 * 2**20),
        name="gram",
    )(*parts)


def pairs(target):
    out = []
    for z in range(4):
        for x in range(4):
            for y in range(4):
                for c in range(2):
                    tz, tx, ty, tc = target(z, x, y, c)
                    out.append((((z * 4 + x) * 4 + y) * 2 + c, (((tz % 4) * 4 + tx % 4) * 4 + ty % 4) * 2 + tc))
    return out


def send(x, target):
    return lax.ppermute(x, AXES, pairs(target))


def first_axis(off):
    return lambda z, x, y, c: (z, x + off * (1 - c), y + off * c, c)


def second_axis(off):
    return lambda z, x, y, c: (z, x + off * c, y + off * (1 - c), c)


def other_core(z, x, y, c):
    return (z, x, y, 1 - c)


def exchange(parts, axis, order):
    return [parts[0]] + [send(parts[off], axis(off)) for off in order]


def add_halves_kernel(*refs):
    ins, (out, half) = refs[:-2], refs[-2:]
    total = sum(x[...] for x in ins[1:]) + ins[0][...]
    rows = half.shape[0]
    out[...] = total
    half[...] = jnp.where(lax.rem(lax.axis_index("gz"), 2) == 0, total[:rows], total[rows:])


def add_halves(*parts):
    rows, lanes = parts[0].shape
    return pl.pallas_call(
        add_halves_kernel,
        out_shape=[jax.ShapeDtypeStruct((rows, lanes), F32), jax.ShapeDtypeStruct((rows // 2, lanes), F32)],
        compiler_params=pltpu.CompilerParams(vmem_limit_bytes=8 * 2**20),
        name="add_halves",
    )(*parts)


def hear_kernel(whole, half, out):
    rows = half.shape[0]
    out[...] = whole[...]
    mine = pl.ds(pl.multiple_of(lax.rem(lax.axis_index("gz"), 2) * rows, rows), rows)
    out[mine, :] = out[mine, :] + half[...]


def hear(whole, half):
    return pl.pallas_call(
        hear_kernel,
        out_shape=jax.ShapeDtypeStruct(whole.shape, F32),
        compiler_params=pltpu.CompilerParams(vmem_limit_bytes=8 * 2**20),
        name="hear",
    )(whole, half)


def plane_total(part):
    terms = (part, send(part, other_core))
    for along_x in (1, 0):

        def whole(z, x, y, c):
            step = 2 - c
            return (z, x + step * along_x, y + step * (1 - along_x), c)

        def shared(z, x, y, c):
            return (z, x + 3 * along_x, y + 3 * (1 - along_x), c)

        part, half = add_halves(*terms)
        heard = hear(send(part, whole), send(half, shared))
        terms = (part, heard, send(heard, other_core))
    return sum(terms)


def body(field, basis_two, basis_three):
    field = field.reshape(4, 2, 16, 2, 64, 256)
    halves = project(field, basis_two.T, basis_three)
    received = [send(theirs, other_core) for _, theirs in halves]
    groups = []
    for (mine, _), part in zip(halves, received):
        groups.append(add_groups(mine, part, groups[-1][:1] if groups else []))
    groups = sum_groups([exchange(part, first_axis, order) for part, order in zip(groups, FIRST)])
    rows = finish(exchange(groups, second_axis, SECOND))
    gathered = [rows] + [send(rows, lambda z, x, y, c, off=off: (z - off, x, y, c)) for off in OFFSETS[1:]]
    return (copy(rows), plane_total(gram_part(gathered)))


def solution(mesh):
    placed = (P(None, "gx", "gz", "gy"), P("gy", None), P("gz", None))
    return jax.shard_map(
        body,
        mesh=mesh,
        in_specs=placed,
        out_specs=(P("gx", ("gy", "gz")), P("gx", None)),
        check_vma=False,
    )
```

```python
import functools

import jax
import jax.numpy as jnp
from jax import lax
from jax.experimental import pallas as pl
from jax.experimental.pallas import tpu as pltpu
from jax.sharding import PartitionSpec as P

V = 4
R = 64
OFFSETS = (0, 1, 2, 3)
FIRST = ((1, 3, 2), (1, 3, 2))
SECOND = (1, 2, 3)
AXES = ("gx", "gy", "gz")
F32, BF16 = jnp.float32, jnp.bfloat16
SIZES = (8, 8)


def split(x):
    hi = x.astype(BF16)
    return hi, (x - hi.astype(F32)).astype(BF16)


def dot(a, b, contract):
    return lax.dot_general(a, b, ((contract[:1], contract[1:]), ((), ())), preferred_element_type=F32)


def contract(cells, w2, w3, mine, theirs):
    size = cells.shape[1]
    quads = [
        jnp.concatenate([cells[i, m, 0], cells[i, m, 1]], axis=1) for m in range(size) for i in range(2)
    ]
    hi, lo = split(jnp.concatenate(quads, axis=0))
    both = dot(hi, w2[...], (1, 0))
    first = both[:, :128] + both[:, 128:] + dot(lo, w2[:, :128], (1, 0))
    for m in range(size):
        hi, lo = split(first[m * 128 : (m + 1) * 128].T)
        core = dot(jnp.concatenate([hi, lo, hi], axis=1), w3[...], (1, 0))
        for r in range(2):
            lanes = slice((2 * m + r) * 128, (2 * m + r + 1) * 128)
            mine[:, :, lanes] = core[r * 64 : r * 64 + 32].reshape(4, 8, 128)
            theirs[:, :, lanes] = core[r * 64 + 32 : r * 64 + 64].reshape(4, 8, 128)


def first_part_kernel(field, b2t_in, b3_in, mine, theirs, later, w2, w3, cells, b2t, b3, rows, sem, small_sem):
    x, gz = lax.axis_index("gy"), lax.axis_index("gz")
    small = [pltpu.make_async_copy(b2t_in, b2t, small_sem.at[0]), pltpu.make_async_copy(b3_in, b3, small_sem.at[1])]
    for copy in small:
        copy.start()

    def load(n):
        part, off = n // 4, n % 4
        cut = pl.ds(part * SIZES[0], SIZES[part])
        to = later if part else cells
        return pltpu.make_async_copy(field.at[lax.rem(x + off, 4), :, cut], to.at[off], sem.at[n])

    load(0).start()
    for copy in small:
        copy.wait()

    for other in range(2):
        for off in range(4):
            start = (lax.rem(gz // 2 + off, 4) * 2 + lax.rem(gz + other, 2)) * 8
            rows[pl.ds((other * 4 + off) * 8, 8), :] = b2t[pl.ds(pl.multiple_of(start, 8), 8), :]
    hi, lo = split(rows[...].T)
    zero = jnp.zeros_like(hi)
    w2[0:256, :] = jnp.concatenate([hi, zero, lo, zero], axis=1)
    w2[256:512, :] = jnp.concatenate([zero, hi, zero, lo], axis=1)
    tall = jnp.concatenate([jnp.concatenate([b3[...]] * 2, axis=1)] * 2, axis=0)
    block = [lax.broadcasted_iota(jnp.int32, (128, 128), i) // 64 for i in range(2)]
    hi, lo = split(jnp.where(block[0] == block[1], tall, 0.0))
    w3[0:128, :] = hi
    w3[128:256, :] = hi
    w3[256:384, :] = lo

    load(1).start()
    for off, ahead in enumerate(((2, 3), (4, 5), (6,), ())):
        load(off).wait()
        for n in ahead:
            load(n).start()
        contract(cells.at[off], w2, w3, mine.at[off], theirs.at[off])
    for n in range(4, 7):
        load(n).wait()


def second_part_kernel(field, early, w2, w3, mine, theirs, late, sem):
    x = lax.axis_index("gy")

    def load():
        cut = pl.ds(SIZES[0], SIZES[1])
        return pltpu.make_async_copy(field.at[lax.rem(x + 3, 4), :, cut], late, sem)

    load().start()
    for off in range(4):
        if off == 3:
            load().wait()
        contract(early.at[off] if off < 3 else late, w2, w3, mine.at[off], theirs.at[off])


def project(field, b2t, b3):
    parts = [jax.ShapeDtypeStruct((4, 4, 8, size * 256), F32) for size in SIZES]
    cells = [(4, 2, size, 2, 64, 256) for size in SIZES]
    costs = [pl.CostEstimate(flops=size * 10**9, bytes_accessed=size * 2**20, transcendentals=0) for size in SIZES]
    params = pltpu.CompilerParams(vmem_limit_bytes=26 * 2**20)
    vmem = pl.BlockSpec(memory_space=pltpu.VMEM)
    field, b2t, b3 = (pltpu.with_memory_space_constraint(a, pltpu.HBM) for a in (field, b2t, b3))
    mine, theirs, later, w2, w3 = pl.pallas_call(
        first_part_kernel,
        out_shape=(
            parts[0],
            parts[0],
            jax.ShapeDtypeStruct((3, *cells[1][1:]), F32),
            jax.ShapeDtypeStruct((512, 256), BF16),
            jax.ShapeDtypeStruct((384, 128), BF16),
        ),
        in_specs=[pl.BlockSpec(memory_space=pltpu.HBM)] * 3,
        out_specs=[vmem] * 5,
        scratch_shapes=[
            pltpu.VMEM(cells[0], F32),
            pltpu.VMEM((64, 256), F32),
            pltpu.VMEM((64, 64), F32),
            pltpu.VMEM((64, 256), F32),
            pltpu.SemaphoreType.DMA((7,)),
            pltpu.SemaphoreType.DMA((2,)),
        ],
        compiler_params=params,
        cost_estimate=costs[0],
        name="project_first_part",
    )(field, b2t, b3)
    second = pl.pallas_call(
        second_part_kernel,
        out_shape=(parts[1], parts[1]),
        in_specs=[pl.BlockSpec(memory_space=pltpu.HBM)] + [vmem] * 3,
        out_specs=[vmem] * 2,
        scratch_shapes=[pltpu.VMEM(cells[1][1:], F32), pltpu.SemaphoreType.DMA],
        compiler_params=params,
        cost_estimate=costs[1],
        name="project_second_part",
    )(field, later, w2, w3)
    return (mine, theirs), second


def add_kernel(mine, received, *rest):
    outs = rest[-4:]
    core = lax.rem(lax.axis_index("gz"), 2)
    for g in range(4):
        for h in range(4):
            v, y = g + (h - g) * core, h + (g - h) * core
            outs[g][h] = mine[v, y] + received[v, y]


def add_groups(mine, received, after):
    vmem = pl.BlockSpec(memory_space=pltpu.VMEM)
    return pl.pallas_call(
        add_kernel,
        in_specs=[vmem] * 2 + [pl.BlockSpec(memory_space=pl.ANY)] * len(after),
        out_shape=[jax.ShapeDtypeStruct(mine.shape[1:], F32)] * 4,
        compiler_params=pltpu.CompilerParams(vmem_limit_bytes=8 * 2**20),
        name="add_cores",
    )(mine, received, *after)


def sum_kernel(*refs):
    ins, outs = refs[:-4], refs[-4:]
    lane = 0
    for p in range(0, len(ins), 4):
        a, b, c, d = ins[p : p + 4]
        lanes = slice(lane, lane + a.shape[-1])
        lane += a.shape[-1]
        for h in range(4):
            outs[h][:, lanes] = (a[h] + b[h]) + (c[h] + d[h])


def sum_groups(parts):
    return pl.pallas_call(
        sum_kernel,
        out_shape=[jax.ShapeDtypeStruct((8, 4096), F32)] * 4,
        compiler_params=pltpu.CompilerParams(vmem_limit_bytes=8 * 2**20),
        name="sum_first_axis",
    )(*[x for part in parts for x in part])


def finish_kernel(a, b, c, d, out):
    total = (a[...] + b[...]) + (c[...] + d[...])
    pairs = total.shape[1] // 128
    rows = total.reshape(8, pairs, 128)
    low = lax.broadcasted_iota(jnp.int32, (pairs, 128), 1) < 64
    for j in range(4):
        even, odd = rows[2 * j], rows[2 * j + 1]
        lanes = slice(j * 128, (j + 1) * 128)
        out[0:pairs, lanes] = jnp.where(low, even, pltpu.roll(odd, 64, 1))
        out[pairs : 2 * pairs, lanes] = jnp.where(low, pltpu.roll(even, 64, 1), odd)


def finish(parts):
    return pl.pallas_call(
        finish_kernel,
        out_shape=jax.ShapeDtypeStruct((parts[0].shape[1] // 64, 512), F32),
        compiler_params=pltpu.CompilerParams(vmem_limit_bytes=8 * 2**20),
        name="sum_second_axis",
    )(*parts)


def copy_kernel(x, out):
    out[...] = x[...]


def copy(x):
    return pl.pallas_call(
        copy_kernel,
        out_shape=jax.ShapeDtypeStruct(x.shape, x.dtype),
        compiler_params=pltpu.CompilerParams(vmem_limit_bytes=8 * 2**20),
        name="copy",
    )(x)


def gram_kernel(a, b, c, d, out, cols):
    z = lax.axis_index("gx")
    for off, ref in zip(OFFSETS, (a, b, c, d)):
        start = pl.multiple_of(lax.rem(z + off, 4) * 64, 64)
        cols[pl.ds(start, 64), :] = ref[...]
    hi, lo = split(a[...])
    chi, clo = split(cols[...])
    both = dot(jnp.concatenate([hi, lo], axis=0), chi, (1, 1))
    out[...] = (both[:64] + both[64:] + dot(hi, clo, (1, 1))) * (1.0 / (V * R * R))


def gram_part(parts):
    return pl.pallas_call(
        gram_kernel,
        out_shape=jax.ShapeDtypeStruct((64, 256), F32),
        scratch_shapes=[pltpu.VMEM((256, 512), F32)],
        compiler_params=pltpu.CompilerParams(vmem_limit_bytes=8 * 2**20),
        name="gram",
    )(*parts)


def pairs(target):
    out = []
    for z in range(4):
        for x in range(4):
            for y in range(4):
                for c in range(2):
                    tz, tx, ty, tc = target(z, x, y, c)
                    out.append((((z * 4 + x) * 4 + y) * 2 + c, (((tz % 4) * 4 + tx % 4) * 4 + ty % 4) * 2 + tc))
    return out


def send(x, target):
    return lax.ppermute(x, AXES, pairs(target))


def first_axis(off):
    return lambda z, x, y, c: (z, x + off * (1 - c), y + off * c, c)


def second_axis(off):
    return lambda z, x, y, c: (z, x + off * c, y + off * (1 - c), c)


def other_core(z, x, y, c):
    return (z, x, y, 1 - c)


def exchange(parts, axis, order):
    return [parts[0]] + [send(parts[off], axis(off)) for off in order]


def add_halves_kernel(*refs):
    ins, (out, half) = refs[:-2], refs[-2:]
    total = sum(x[...] for x in ins[1:]) + ins[0][...]
    rows = half.shape[0]
    out[...] = total
    half[...] = jnp.where(lax.rem(lax.axis_index("gz"), 2) == 0, total[:rows], total[rows:])


def add_halves(*parts):
    rows, lanes = parts[0].shape
    return pl.pallas_call(
        add_halves_kernel,
        out_shape=[jax.ShapeDtypeStruct((rows, lanes), F32), jax.ShapeDtypeStruct((rows // 2, lanes), F32)],
        compiler_params=pltpu.CompilerParams(vmem_limit_bytes=8 * 2**20),
        name="add_halves",
    )(*parts)


def hear_kernel(whole, half, out):
    rows = half.shape[0]
    out[...] = whole[...]
    mine = pl.ds(pl.multiple_of(lax.rem(lax.axis_index("gz"), 2) * rows, rows), rows)
    out[mine, :] = out[mine, :] + half[...]


def hear(whole, half):
    return pl.pallas_call(
        hear_kernel,
        out_shape=jax.ShapeDtypeStruct(whole.shape, F32),
        compiler_params=pltpu.CompilerParams(vmem_limit_bytes=8 * 2**20),
        name="hear",
    )(whole, half)


def plane_total(part):
    terms = (part, send(part, other_core))
    for along_x in (1, 0):

        def whole(z, x, y, c):
            step = 1 + c
            return (z, x + step * along_x, y + step * (1 - along_x), c)

        def shared(z, x, y, c):
            return (z, x + 3 * along_x, y + 3 * (1 - along_x), c)

        part, half = add_halves(*terms)
        heard = hear(send(part, whole), send(half, shared))
        terms = (part, heard, send(heard, other_core))
    return sum(terms)


def body(field, basis_two, basis_three):
    field = field.reshape(4, 2, 16, 2, 64, 256)
    halves = project(field, basis_two.T, basis_three)
    received = [send(theirs, other_core) for _, theirs in halves]
    groups = []
    for (mine, _), part in zip(halves, received):
        groups.append(add_groups(mine, part, groups[-1][:1] if groups else []))
    groups = sum_groups([exchange(part, first_axis, order) for part, order in zip(groups, FIRST)])
    rows = finish(exchange(groups, second_axis, SECOND))
    gathered = [rows] + [send(rows, lambda z, x, y, c, off=off: (z - off, x, y, c)) for off in OFFSETS[1:]]
    return (copy(rows), plane_total(gram_part(gathered)))


def solution(mesh):
    placed = (P(None, "gx", "gz", "gy"), P("gy", None), P("gz", None))
    return jax.shard_map(
        body,
        mesh=mesh,
        in_specs=placed,
        out_specs=(P("gx", ("gy", "gz")), P("gx", None)),
        check_vma=False,
    )
```

```python
import functools

import jax
import jax.numpy as jnp
from jax import lax
from jax.experimental import pallas as pl
from jax.experimental.pallas import tpu as pltpu
from jax.sharding import PartitionSpec as P

V = 4
R = 64
OFFSETS = (0, 1, 2, 3)
FIRST = ((1, 3, 2), (1, 3, 2))
SECOND = (1, 2, 3)
AXES = ("gx", "gy", "gz")
F32, BF16 = jnp.float32, jnp.bfloat16
SIZES = (8, 8)


def split(x):
    hi = x.astype(BF16)
    return hi, (x - hi.astype(F32)).astype(BF16)


def dot(a, b, contract):
    return lax.dot_general(a, b, ((contract[:1], contract[1:]), ((), ())), preferred_element_type=F32)


def contract(cells, w2, w3, mine, theirs):
    size = cells.shape[1]
    quads = [
        jnp.concatenate([cells[i, m, 0], cells[i, m, 1]], axis=1) for m in range(size) for i in range(2)
    ]
    hi, lo = split(jnp.concatenate(quads, axis=0))
    both = dot(hi, w2[...], (1, 0))
    first = both[:, :128] + both[:, 128:] + dot(lo, w2[:, :128], (1, 0))
    for m in range(size):
        hi, lo = split(first[m * 128 : (m + 1) * 128].T)
        core = dot(jnp.concatenate([hi, lo, hi], axis=1), w3[...], (1, 0))
        for r in range(2):
            lanes = slice((2 * m + r) * 128, (2 * m + r + 1) * 128)
            mine[:, :, lanes] = core[r * 64 : r * 64 + 32].reshape(4, 8, 128)
            theirs[:, :, lanes] = core[r * 64 + 32 : r * 64 + 64].reshape(4, 8, 128)


def first_part_kernel(field, b2t_in, b3_in, mine, theirs, later, w2, w3, cells, b2t, b3, rows, sem, small_sem):
    x, gz = lax.axis_index("gy"), lax.axis_index("gz")
    small = [pltpu.make_async_copy(b2t_in, b2t, small_sem.at[0]), pltpu.make_async_copy(b3_in, b3, small_sem.at[1])]
    for copy in small:
        copy.start()

    def load(n):
        part, off = n // 4, n % 4
        cut = pl.ds(part * SIZES[0], SIZES[part])
        to = later if part else cells
        return pltpu.make_async_copy(field.at[lax.rem(x + off, 4), :, cut], to.at[off], sem.at[n])

    load(0).start()
    for copy in small:
        copy.wait()

    for other in range(2):
        for off in range(4):
            start = (lax.rem(gz // 2 + off, 4) * 2 + lax.rem(gz + other, 2)) * 8
            rows[pl.ds((other * 4 + off) * 8, 8), :] = b2t[pl.ds(pl.multiple_of(start, 8), 8), :]
    hi, lo = split(rows[...].T)
    zero = jnp.zeros_like(hi)
    w2[0:256, :] = jnp.concatenate([hi, zero, lo, zero], axis=1)
    w2[256:512, :] = jnp.concatenate([zero, hi, zero, lo], axis=1)
    tall = jnp.concatenate([jnp.concatenate([b3[...]] * 2, axis=1)] * 2, axis=0)
    block = [lax.broadcasted_iota(jnp.int32, (128, 128), i) // 64 for i in range(2)]
    hi, lo = split(jnp.where(block[0] == block[1], tall, 0.0))
    w3[0:128, :] = hi
    w3[128:256, :] = hi
    w3[256:384, :] = lo

    load(1).start()
    for off, ahead in enumerate(((2, 3), (4, 5, 6), (), ())):
        load(off).wait()
        for n in ahead:
            load(n).start()
        contract(cells.at[off], w2, w3, mine.at[off], theirs.at[off])
    for n in range(4, 7):
        load(n).wait()


def second_part_kernel(field, early, w2, w3, mine, theirs, late, sem):
    x = lax.axis_index("gy")

    def load():
        cut = pl.ds(SIZES[0], SIZES[1])
        return pltpu.make_async_copy(field.at[lax.rem(x + 3, 4), :, cut], late, sem)

    load().start()
    for off in range(4):
        if off == 3:
            load().wait()
        contract(early.at[off] if off < 3 else late, w2, w3, mine.at[off], theirs.at[off])


def project(field, b2t, b3):
    parts = [jax.ShapeDtypeStruct((4, 4, 8, size * 256), F32) for size in SIZES]
    cells = [(4, 2, size, 2, 64, 256) for size in SIZES]
    costs = [pl.CostEstimate(flops=size * 10**9, bytes_accessed=size * 2**20, transcendentals=0) for size in SIZES]
    params = pltpu.CompilerParams(vmem_limit_bytes=26 * 2**20)
    vmem = pl.BlockSpec(memory_space=pltpu.VMEM)
    field, b2t, b3 = (pltpu.with_memory_space_constraint(a, pltpu.HBM) for a in (field, b2t, b3))
    mine, theirs, later, w2, w3 = pl.pallas_call(
        first_part_kernel,
        out_shape=(
            parts[0],
            parts[0],
            jax.ShapeDtypeStruct((3, *cells[1][1:]), F32),
            jax.ShapeDtypeStruct((512, 256), BF16),
            jax.ShapeDtypeStruct((384, 128), BF16),
        ),
        in_specs=[pl.BlockSpec(memory_space=pltpu.HBM)] * 3,
        out_specs=[vmem] * 5,
        scratch_shapes=[
            pltpu.VMEM(cells[0], F32),
            pltpu.VMEM((64, 256), F32),
            pltpu.VMEM((64, 64), F32),
            pltpu.VMEM((64, 256), F32),
            pltpu.SemaphoreType.DMA((7,)),
            pltpu.SemaphoreType.DMA((2,)),
        ],
        compiler_params=params,
        cost_estimate=costs[0],
        name="project_first_part",
    )(field, b2t, b3)
    second = pl.pallas_call(
        second_part_kernel,
        out_shape=(parts[1], parts[1]),
        in_specs=[pl.BlockSpec(memory_space=pltpu.HBM)] + [vmem] * 3,
        out_specs=[vmem] * 2,
        scratch_shapes=[pltpu.VMEM(cells[1][1:], F32), pltpu.SemaphoreType.DMA],
        compiler_params=params,
        cost_estimate=costs[1],
        name="project_second_part",
    )(field, later, w2, w3)
    return (mine, theirs), second


def add_kernel(mine, received, *rest):
    outs = rest[-4:]
    core = lax.rem(lax.axis_index("gz"), 2)
    for g in range(4):
        for h in range(4):
            v, y = g + (h - g) * core, h + (g - h) * core
            outs[g][h] = mine[v, y] + received[v, y]


def add_groups(mine, received, after):
    vmem = pl.BlockSpec(memory_space=pltpu.VMEM)
    return pl.pallas_call(
        add_kernel,
        in_specs=[vmem] * 2 + [pl.BlockSpec(memory_space=pl.ANY)] * len(after),
        out_shape=[jax.ShapeDtypeStruct(mine.shape[1:], F32)] * 4,
        compiler_params=pltpu.CompilerParams(vmem_limit_bytes=8 * 2**20),
        name="add_cores",
    )(mine, received, *after)


def sum_kernel(*refs):
    ins, outs = refs[:-4], refs[-4:]
    lane = 0
    for p in range(0, len(ins), 4):
        a, b, c, d = ins[p : p + 4]
        lanes = slice(lane, lane + a.shape[-1])
        lane += a.shape[-1]
        for h in range(4):
            outs[h][:, lanes] = (a[h] + b[h]) + (c[h] + d[h])


def sum_groups(parts):
    return pl.pallas_call(
        sum_kernel,
        out_shape=[jax.ShapeDtypeStruct((8, 4096), F32)] * 4,
        compiler_params=pltpu.CompilerParams(vmem_limit_bytes=8 * 2**20),
        name="sum_first_axis",
    )(*[x for part in parts for x in part])


def finish_kernel(a, b, c, d, out):
    total = (a[...] + b[...]) + (c[...] + d[...])
    pairs = total.shape[1] // 128
    rows = total.reshape(8, pairs, 128)
    low = lax.broadcasted_iota(jnp.int32, (pairs, 128), 1) < 64
    for j in range(4):
        even, odd = rows[2 * j], rows[2 * j + 1]
        lanes = slice(j * 128, (j + 1) * 128)
        out[0:pairs, lanes] = jnp.where(low, even, pltpu.roll(odd, 64, 1))
        out[pairs : 2 * pairs, lanes] = jnp.where(low, pltpu.roll(even, 64, 1), odd)


def finish(parts):
    return pl.pallas_call(
        finish_kernel,
        out_shape=jax.ShapeDtypeStruct((parts[0].shape[1] // 64, 512), F32),
        compiler_params=pltpu.CompilerParams(vmem_limit_bytes=8 * 2**20),
        name="sum_second_axis",
    )(*parts)


def copy_kernel(x, out):
    out[...] = x[...]


def copy(x):
    return pl.pallas_call(
        copy_kernel,
        out_shape=jax.ShapeDtypeStruct(x.shape, x.dtype),
        compiler_params=pltpu.CompilerParams(vmem_limit_bytes=8 * 2**20),
        name="copy",
    )(x)


def gram_kernel(a, b, c, d, out, cols):
    z = lax.axis_index("gx")
    for off, ref in zip(OFFSETS, (a, b, c, d)):
        start = pl.multiple_of(lax.rem(z + off, 4) * 64, 64)
        cols[pl.ds(start, 64), :] = ref[...]
    hi, lo = split(a[...])
    chi, clo = split(cols[...])
    both = dot(jnp.concatenate([hi, lo], axis=0), chi, (1, 1))
    out[...] = (both[:64] + both[64:] + dot(hi, clo, (1, 1))) * (1.0 / (V * R * R))


def gram_part(parts):
    return pl.pallas_call(
        gram_kernel,
        out_shape=jax.ShapeDtypeStruct((64, 256), F32),
        scratch_shapes=[pltpu.VMEM((256, 512), F32)],
        compiler_params=pltpu.CompilerParams(vmem_limit_bytes=8 * 2**20),
        name="gram",
    )(*parts)


def pairs(target):
    out = []
    for z in range(4):
        for x in range(4):
            for y in range(4):
                for c in range(2):
                    tz, tx, ty, tc = target(z, x, y, c)
                    out.append((((z * 4 + x) * 4 + y) * 2 + c, (((tz % 4) * 4 + tx % 4) * 4 + ty % 4) * 2 + tc))
    return out


def send(x, target):
    return lax.ppermute(x, AXES, pairs(target))


def first_axis(off):
    return lambda z, x, y, c: (z, x + off * (1 - c), y + off * c, c)


def second_axis(off):
    return lambda z, x, y, c: (z, x + off * c, y + off * (1 - c), c)


def other_core(z, x, y, c):
    return (z, x, y, 1 - c)


def exchange(parts, axis, order):
    return [parts[0]] + [send(parts[off], axis(off)) for off in order]


def add_halves_kernel(*refs):
    ins, (out, half) = refs[:-2], refs[-2:]
    total = sum(x[...] for x in ins[1:]) + ins[0][...]
    rows = half.shape[0]
    out[...] = total
    half[...] = jnp.where(lax.rem(lax.axis_index("gz"), 2) == 0, total[:rows], total[rows:])


def add_halves(*parts):
    rows, lanes = parts[0].shape
    return pl.pallas_call(
        add_halves_kernel,
        out_shape=[jax.ShapeDtypeStruct((rows, lanes), F32), jax.ShapeDtypeStruct((rows // 2, lanes), F32)],
        compiler_params=pltpu.CompilerParams(vmem_limit_bytes=8 * 2**20),
        name="add_halves",
    )(*parts)


def hear_kernel(whole, half, out):
    rows = half.shape[0]
    out[...] = whole[...]
    mine = pl.ds(pl.multiple_of(lax.rem(lax.axis_index("gz"), 2) * rows, rows), rows)
    out[mine, :] = out[mine, :] + half[...]


def hear(whole, half):
    return pl.pallas_call(
        hear_kernel,
        out_shape=jax.ShapeDtypeStruct(whole.shape, F32),
        compiler_params=pltpu.CompilerParams(vmem_limit_bytes=8 * 2**20),
        name="hear",
    )(whole, half)


def plane_total(part):
    terms = (part, send(part, other_core))
    for along_x in (0, 1):

        def whole(z, x, y, c):
            step = 1 + c
            return (z, x + step * along_x, y + step * (1 - along_x), c)

        def shared(z, x, y, c):
            return (z, x + 3 * along_x, y + 3 * (1 - along_x), c)

        part, half = add_halves(*terms)
        heard = hear(send(part, whole), send(half, shared))
        terms = (part, heard, send(heard, other_core))
    return sum(terms)


def body(field, basis_two, basis_three):
    field = field.reshape(4, 2, 16, 2, 64, 256)
    halves = project(field, basis_two.T, basis_three)
    received = [send(theirs, other_core) for _, theirs in halves]
    groups = []
    for (mine, _), part in zip(halves, received):
        groups.append(add_groups(mine, part, groups[-1][:1] if groups else []))
    groups = sum_groups([exchange(part, first_axis, order) for part, order in zip(groups, FIRST)])
    rows = finish(exchange(groups, second_axis, SECOND))
    gathered = [rows] + [send(rows, lambda z, x, y, c, off=off: (z - off, x, y, c)) for off in OFFSETS[1:]]
    return (copy(rows), plane_total(gram_part(gathered)))


def solution(mesh):
    placed = (P(None, "gx", "gz", "gy"), P("gy", None), P("gz", None))
    return jax.shard_map(
        body,
        mesh=mesh,
        in_specs=placed,
        out_specs=(P("gx", ("gy", "gz")), P("gx", None)),
        check_vma=False,
    )
```
